256 devices in a mesh: rep: 8 (over x, y_hi), fsdp: 32 (over z, y_lo, core).
Axes of the slice: x: 4, y: 4 (y_hi: 2, y_lo: 2; y = y_hi * 2 + y_lo), z: 8, core: 2. Of those that a mesh axis runs over, the one named last changes fastest.
Arguments:
- tokens: bfloat16 [8, 2048, 2048], P('rep', 'fsdp'), may hold values from -6 to 6
- cotangent: bfloat16 [8, 2048, 2048], P('rep', 'fsdp'), may hold values from -6 to 6
- gain: float32 [8, 2048], P('rep'), may hold values from 0.1 to 1.9
- w_gate: float32 [8, 2048, 4096], P('rep', None, 'fsdp'), may hold values from -5 to 5
- w_up: float32 [8, 2048, 4096], P('rep', None, 'fsdp'), may hold values from -5 to 5
- w_down: float32 [8, 4096, 2048], P('rep', 'fsdp'), may hold values from -5 to 5
- step_index: int32 [1], replicated, may hold values from 0 to 999
Outputs:
- input_grad: bfloat16 [8, 2048, 2048], P('rep', 'fsdp')
- new_gain: float32 [8, 2048], P('rep')
- new_gate: float32 [8, 2048, 4096], P('rep', None, 'fsdp')
- new_up: float32 [8, 2048, 4096], P('rep', None, 'fsdp')
- new_down: float32 [8, 4096, 2048], P('rep', 'fsdp')
The draws below stay inside these ranges and needn't reach their ends.
All inputs are finite; a program needn't handle non-finite values.
Results may differ from the reference program's by a relative error of at most 0.025.
Values may be sent and summed in bfloat16 or wider, within the bound.
A program may use at most 128 MiB of HBM per device.

```python
import jax
import jax.numpy as jnp
from jax import lax

D = 2048
FF = 4096
TOK_REP = 2048
N_REP = 8
N_FSDP = 32


def with_spikes(result, key, source, target, blocks, factor):
    def block_of(dim):
        return (jnp.arange(result.shape[dim]) // (result.shape[dim] // blocks)).reshape((-1,) + (1,) * (result.ndim - 1 - dim))

    one_side = jax.random.permutation(key, blocks)[block_of(target)]
    second = (block_of(target) + blocks // 2) % blocks
    return jnp.where((block_of(source) == one_side) | (block_of(source) == second), factor * result, result)


def shard_levels(rng, shape, split, least, top_value):
    factor_of = 1.0
    for axis_at, parts in split:
        heights = jax.random.uniform(jax.random.fold_in(jax.random.fold_in(rng, 6), axis_at), (parts,), jnp.float32, least / len(split), top_value / len(split))
        factor_of = factor_of * jnp.repeat(jnp.exp(heights), shape[axis_at] // parts).reshape((-1,) + (1,) * (len(shape) - 1 - axis_at))
    return factor_of


def centred(rng, extent, scale, bound, split=(), kind=jnp.bfloat16):
    level = shard_levels(rng, extent, split, -0.22, 0.18) if split else 1.0
    values = jax.random.normal(rng, extent, jnp.float32) * scale * level
    return jnp.minimum(jnp.maximum(values, -bound), bound).astype(kind)


def noise_with(stream_key, extent, width, limit, shards, heavy, held_as=jnp.bfloat16):
    result = width * jax.random.normal(stream_key, extent, jnp.float32)
    if shards:
        result = result * shard_levels(stream_key, extent, shards, -0.22, 0.18)
    return jnp.clip(with_spikes(result, jax.random.fold_in(stream_key, 3), *heavy), -limit, limit).astype(held_as)


def setup_inputs(seed: int = 0) -> dict:
    seeds = jax.random.split(jax.random.key(seed), 8)
    tokens = centred(seeds[0], (N_REP, TOK_REP, D), 1.0, 6.0, ((0, 8), (1, 32)))
    cotangent = noise_with(seeds[1], (N_REP, TOK_REP, D), 1.0, 6.0, ((0, 8), (1, 32)), (1, 2, 32, 2.75))
    gain = jnp.clip(1.0 + 0.18 * jax.random.normal(seeds[2], (N_REP, D), jnp.float32), 0.1, 1.9)
    w_gate = centred(seeds[3], (N_REP, D, FF), 1.0, 5.0, ((0, 8), (2, 32)), jnp.float32)
    w_up = centred(seeds[4], (N_REP, D, FF), 1.0, 5.0, ((0, 8), (2, 32)), jnp.float32)
    w_down = centred(seeds[5], (N_REP, FF, D), 1.0, 5.0, ((0, 8), (1, 32)), jnp.float32)
    step_index = jax.random.randint(seeds[6], (1,), 0, 1000).astype(jnp.int32)
    return {"tokens": tokens, "cotangent": cotangent, "gain": gain, "w_gate": w_gate, "w_up": w_up, "w_down": w_down, "step_index": step_index}


learn_rate = 0.02
epsilon = 1e-05

def to_bf16_f32(array):
    rounded = array.astype(jnp.bfloat16)
    rounded = lax.optimization_barrier(rounded)
    return rounded.astype(jnp.float32)

def replica_step(tokens_r, cotangent_r, gain_r, gate_r, up_r, down_r):
    in_scale = D ** (-0.5)
    out_scale = FF ** (-0.5)
    local_units = FF // N_FSDP
    values = tokens_r.astype(jnp.float32)
    inv_rms = lax.rsqrt(lax.optimization_barrier(jnp.mean(values * values, axis=1, keepdims=True)) + epsilon)
    unit_rows = values * inv_rms
    normed = (unit_rows * gain_r).astype(jnp.bfloat16)
    gate_b = gate_r.astype(jnp.bfloat16)
    up_b = up_r.astype(jnp.bfloat16)
    down_b = down_r.astype(jnp.bfloat16)
    gate_pre = jnp.dot(normed, gate_b, preferred_element_type=jnp.float32) * in_scale
    up_pre = jnp.dot(normed, up_b, preferred_element_type=jnp.float32) * in_scale
    sigmoid_gate = jax.nn.sigmoid(gate_pre)
    activated = gate_pre * sigmoid_gate
    hidden = (activated * up_pre).astype(jnp.bfloat16)
    grad_down = jnp.dot(hidden.T, cotangent_r, preferred_element_type=jnp.float32) * out_scale
    grad_hidden = jnp.dot(cotangent_r, down_b.T, preferred_element_type=jnp.float32) * out_scale
    grad_gate = (grad_hidden * up_pre * sigmoid_gate * (1.0 + gate_pre * (1.0 - sigmoid_gate))).astype(jnp.bfloat16)
    grad_up = (grad_hidden * activated).astype(jnp.bfloat16)
    grad_wgate = jnp.dot(normed.T, grad_gate, preferred_element_type=jnp.float32) * in_scale
    grad_wup = jnp.dot(normed.T, grad_up, preferred_element_type=jnp.float32) * in_scale
    gate_blocks = grad_gate.astype(jnp.float32).reshape(TOK_REP, N_FSDP, local_units)
    up_blocks = grad_up.astype(jnp.float32).reshape(TOK_REP, N_FSDP, local_units)
    wgate_blocks = gate_b.astype(jnp.float32).reshape(D, N_FSDP, local_units)
    wup_blocks = up_b.astype(jnp.float32).reshape(D, N_FSDP, local_units)
    back_terms = jnp.einsum('tnp,dnp->ntd', gate_blocks, wgate_blocks)
    back_terms = (back_terms + jnp.einsum('tnp,dnp->ntd', up_blocks, wup_blocks)) * in_scale
    grad_normed = lax.optimization_barrier(jnp.sum(to_bf16_f32(back_terms), axis=0))
    grad_gain = lax.optimization_barrier(jnp.sum(grad_normed * unit_rows, axis=0))
    scaled = grad_normed * gain_r
    input_grad = cotangent_r.astype(jnp.float32) + inv_rms * (scaled - unit_rows * lax.optimization_barrier(jnp.mean(scaled * unit_rows, axis=1, keepdims=True)))
    input_grad = input_grad.astype(jnp.bfloat16)
    return (input_grad, gain_r - learn_rate * grad_gain, gate_r - learn_rate * grad_wgate, up_r - learn_rate * grad_wup, down_r - learn_rate * grad_down)

def reference(tokens, cotangent, gain, w_gate, w_up, w_down, step_index):
    results = [replica_step(tokens[replica], cotangent[replica], gain[replica], w_gate[replica], w_up[replica], w_down[replica]) for replica in range(N_REP)]
    stacked = [jnp.stack([item[column] for item in results]) for column in range(5)]
    level_count = N_REP.bit_length() - 1
    level = step_index[0] % level_count
    partner = jnp.bitwise_xor(jnp.arange(N_REP, dtype=jnp.int32), jnp.left_shift(jnp.int32(1), level).astype(jnp.int32))
    mixed = [0.5 * (array + jnp.take(array, partner, axis=0)) for array in stacked[1:]]
    return (stacked[0], mixed[0], mixed[1], mixed[2], mixed[3])
```

```python
import functools

import jax
import jax.numpy as jnp
from jax import lax
from jax.experimental import pallas as pl
from jax.experimental.pallas import tpu as pltpu
from jax.sharding import PartitionSpec as P

MESH = pl.DeviceIdType.MESH
F32 = jnp.float32
BF16 = jnp.bfloat16

learn_rate = 0.02
epsilon = 1e-05

NT = (((1,), (1,)), ((), ()))
NN = (((1,), (0,)), ((), ()))

OWN, FOUR = 6, 7
WIDTH = 512


def slot_of(direction, step):
    if step == 0:
        return OWN
    return 2 * (step - 1) + direction


def kernel(
    level,
    tok_hbm, cot_hbm, gain_hbm, wg_hbm, wu_hbm, wd_hbm,
    ig_out, gain_out, ng_out, nu_out, nd_out,
    tok, gain, raw, wt, wb, normed, cot, back, xt, terms,
    sib_out, sib_in, keep, y_out, y_in, x_out, x_in, rs_out, rs_in,
    gain_one, gain_two, gain_ring, gain_part, gain_new, ig,
    in_sem, out_sem, ag_s, ag_r, w_s, w_r, sib_s, sib_r, y_s, y_r, x_s, x_r,
    rs_s, rs_r, g_s, g_r,
):
    rep = lax.axis_index("rep")
    me = lax.axis_index("fsdp")
    n_fsdp = lax.axis_size("fsdp")
    width = tok.shape[1]
    rows = tok.shape[0]
    units = wt.shape[1]
    pieces = width // WIDTH
    count = 3 * pieces
    in_scale = width ** (-0.5)
    out_scale = (units * n_fsdp) ** (-0.5)

    up = (rep, lax.rem(me + 4, n_fsdp))
    down = (rep, lax.rem(me + n_fsdp - 4, n_fsdp))
    sib = (rep, me + 1 - 2 * lax.rem(me, 2))
    across = (rep, me + 2 - 4 * lax.rem(me // 2, 2))
    far = 1 << level
    partner = (rep + far - 2 * far * lax.rem(rep // far, 2), me)
    ring = (up, down)

    def remote(src, dst, send, recv, device):
        copy = pltpu.make_async_remote_copy(
            src_ref=src, dst_ref=dst, send_sem=send, recv_sem=recv,
            device_id=device, device_id_type=MESH,
        )
        copy.start()
        sent.append(copy)
        return copy

    sent = []

    loads = [
        pltpu.make_async_copy(cot_hbm, cot.at[OWN], in_sem.at[0]),
        pltpu.make_async_copy(tok_hbm, tok, in_sem.at[1]),
        pltpu.make_async_copy(gain_hbm, gain, in_sem.at[2]),
        pltpu.make_async_copy(wg_hbm, raw.at[0], in_sem.at[3]),
        pltpu.make_async_copy(wu_hbm, raw.at[1], in_sem.at[4]),
        pltpu.make_async_copy(wd_hbm, wt.at[2], in_sem.at[5]),
    ]
    for load in loads:
        load.start()

    barrier = pltpu.get_barrier_semaphore()
    for other in (up, down, sib, across, partner):
        pl.semaphore_signal(barrier, inc=1, device_id=other, device_id_type=MESH)
    pl.semaphore_wait(barrier, 5)

    def gather_step(which, buffer, step):
        copies = []
        for direction in (0, 1):
            src = buffer.at[slot_of(direction, step - 1)]
            if step < 4:
                dst = buffer.at[slot_of(direction, step)]
            else:
                half = pl.ds(direction * (rows // 2), rows // 2)
                src = src.at[half]
                dst = buffer.at[FOUR, half]
            copies.append(
                remote(src, dst, ag_s.at[which, direction, step - 1],
                       ag_r.at[which, direction, step - 1], ring[direction])
            )
        return copies

    loads[0].wait()
    cot_copies = gather_step(1, cot, 1)

    loads[1].wait()
    loads[2].wait()
    for r in range(0, rows, 16):
        part = pl.ds(r, 16)
        values = tok[part, :].astype(F32)
        inv_rms = lax.rsqrt(jnp.mean(values * values, axis=1, keepdims=True) + epsilon)
        normed[OWN, part, :] = ((values * inv_rms) * gain[...]).astype(BF16)
    normed_copies = gather_step(0, normed, 1)

    w_copies = []

    def share_weight(m):
        own = wb.at[m, pl.ds(0, units)]
        first = remote(own, wb.at[m, pl.ds(2 * units, units)], w_s.at[m, 0], w_r.at[m, 0], across)
        second = remote(own, wb.at[m, pl.ds(units, units)], w_s.at[m, 1], w_r.at[m, 1], sib)
        w_copies.append((first, second))

    for m in (0, 1):
        loads[3 + m].wait()
        for c in range(0, width, 128):
            turned = raw[m, c:c + 128, :].T
            wt[m, :, c:c + 128] = turned
            wb[m, 0:units, c:c + 128] = turned.astype(BF16)
        share_weight(m)
    loads[5].wait()
    wb[2, 0:units, :] = wt[2].astype(BF16)
    share_weight(2)

    def pass_weight(m):
        w_copies[m][0].wait_recv()
        src = wb.at[m, pl.ds(2 * units, units)]
        return remote(src, wb.at[m, pl.ds(3 * units, units)], w_s.at[m, 2], w_r.at[m, 2], sib)

    def forward(g, tile):
        n_rows = normed[2 * g:2 * g + 2].reshape(2 * rows, width)
        c_rows = cot[2 * g:2 * g + 2].reshape(2 * rows, width)
        cols = slice(tile * 2 * units, (tile + 1) * 2 * units)
        dot = functools.partial(lax.dot_general, dimension_numbers=NT, preferred_element_type=F32)
        gate_pre = dot(n_rows, wb[0, cols, :]) * in_scale
        up_pre = dot(n_rows, wb[1, cols, :]) * in_scale
        grad_hidden = dot(c_rows, wb[2, cols, :]) * out_scale
        sigmoid_gate = jax.nn.sigmoid(gate_pre)
        activated = gate_pre * sigmoid_gate
        hidden = activated * up_pre
        grad_gate = grad_hidden * up_pre * sigmoid_gate * (1.0 + gate_pre * (1.0 - sigmoid_gate))
        grad_up = grad_hidden * activated
        back[0, g, :, cols] = grad_gate.astype(BF16)
        back[1, g, :, cols] = grad_up.astype(BF16)
        lanes = slice(g * 2 * rows, (g + 1) * 2 * rows)
        xt[0, cols, lanes] = grad_gate.T.astype(BF16)
        xt[1, cols, lanes] = grad_up.T.astype(BF16)
        xt[2, cols, lanes] = hidden.T.astype(BF16)

    def term(g):
        for c in range(0, width, WIDTH):
            part = slice(c, c + WIDTH)
            value = lax.dot_general(back[0, g], wb[0, :, part], NN, preferred_element_type=F32)
            value += lax.dot_general(back[1, g], wb[1, :, part], NN, preferred_element_type=F32)
            value = (value * in_scale).astype(BF16)
            terms[2 * g:2 * g + 2, :, part] = value.reshape(2, rows, WIDTH)

    handed = []
    for step in (1, 2, 3):
        for copy in cot_copies:
            copy.wait_recv()
        cot_copies = gather_step(1, cot, step + 1)
        for copy in normed_copies:
            copy.wait_recv()
        normed_copies = gather_step(0, normed, step + 1)
        if step == 1:
            for m in range(3):
                w_copies[m][1].wait_recv()
        forward(step - 1, 0)
        handed.append(pass_weight(step - 1))
    for copy in handed:
        copy.wait_recv()
    for g in range(3):
        forward(g, 1)
    for g in range(3):
        term(g)
    for copy in cot_copies + normed_copies:
        copy.wait_recv()
    forward(3, 0)
    forward(3, 1)

    order = [(m, q) for m in (2, 0, 1) for q in range(pieces)]
    targets = (ng_out, nu_out, nd_out)
    sib_copies, y_copies, x_copies = [], [], []

    def product(i):
        m, q = order[i]
        cols = slice(q * WIDTH, (q + 1) * WIDTH)
        right = (cot if m == 2 else normed)[:, :, cols].reshape(8 * rows, WIDTH)
        scale = out_scale if m == 2 else in_scale
        for tile in (0, 1):
            part = slice(tile * 2 * units, (tile + 1) * 2 * units)
            value = lax.dot_general(xt[m, part, :], right, NN, preferred_element_type=F32) * scale
            keep[i, tile] = value[:units]
            sib_out[i, tile] = value[units:].astype(BF16)
        sib_copies.append(remote(sib_out.at[i], sib_in.at[i], sib_s.at[i], sib_r.at[i], sib))

    def add_sib(i):
        sib_copies[i].wait_recv()
        y_out[i] = (keep[i, 1] + sib_in[i, 1].astype(F32)).astype(BF16)
        y_copies.append(remote(y_out.at[i], y_in.at[i], y_s.at[i], y_r.at[i], across))
        keep[i, 0] += sib_in[i, 0].astype(F32)

    def add_across(i):
        m, q = order[i]
        y_copies[i].wait_recv()
        gradient = keep[i, 0] + y_in[i].astype(F32)
        new = wt[m, :, q * WIDTH:(q + 1) * WIDTH] - learn_rate * gradient
        keep[i, 0] = new
        x_out[i] = new.astype(BF16)
        x_copies.append(remote(x_out.at[i], x_in.at[i], x_s.at[i], x_r.at[i], partner))

    writes = []

    def average(i):
        m, q = order[i]
        x_copies[i].wait_recv()
        keep[i, 0] = 0.5 * (keep[i, 0] + x_in[i].astype(F32))
        write = pltpu.make_async_copy(
            keep.at[i, 0], targets[m].at[:, pl.ds(q * WIDTH, WIDTH)], out_sem.at[i]
        )
        write.start()
        writes.append(write)

    half = rows // 2
    rs_copies = {}

    def scatter_first():
        for direction in (0, 1):
            part = pl.ds(direction * half, half)
            rs_copies[direction] = remote(
                terms.at[FOUR, part], rs_in.at[direction, 0, part],
                rs_s.at[direction, 0], rs_r.at[direction, 0], ring[direction]
            )

    def scatter_step(step):
        for direction in (0, 1):
            rs_copies[direction].wait_recv()
            slot = slot_of(1 - direction, step)
            if step == 3:
                a = direction * half
                b = half - a
                mine = slice(a, a + half)
                rest = slice(b, b + half)
                rs_out[direction, 0, mine] = (
                    terms[slot, mine, :].astype(F32) + rs_in[direction, 0, mine, :].astype(F32)
                ).astype(BF16)
                rs_out[direction, 0, rest] = terms[slot, rest, :]
            else:
                rs_out[direction, 3 - step] = (
                    terms[slot].astype(F32) + rs_in[direction, 3 - step].astype(F32)
                ).astype(BF16)
            rs_copies[direction] = remote(
                rs_out.at[direction, 3 - step], rs_in.at[direction, 4 - step],
                rs_s.at[direction, 4 - step], rs_r.at[direction, 4 - step], ring[direction]
            )

    def scatter_last():
        for direction in (0, 1):
            rs_copies[direction].wait_recv()
        total = jnp.zeros((8, width), F32)
        for r in range(0, rows, 16):
            part = slice(r, r + 16)
            values = tok[part, :].astype(F32)
            inv_rms = lax.rsqrt(jnp.mean(values * values, axis=1, keepdims=True) + epsilon)
            unit = values * inv_rms
            grad = (
                terms[OWN, part, :].astype(F32)
                + rs_in[0, 3, part, :].astype(F32)
                + rs_in[1, 3, part, :].astype(F32)
            )
            product_ = grad * unit
            total += product_[:8] + product_[8:]
            scaled = grad * gain[...]
            mean = jnp.mean(scaled * unit, axis=1, keepdims=True)
            ig[part, :] = (
                cot[OWN, part, :].astype(F32) + inv_rms * (scaled - unit * mean)
            ).astype(BF16)
        gain_one[0] = total
        write = pltpu.make_async_copy(ig, ig_out, out_sem.at[count])
        write.start()
        writes.append(write)

    gain_copies = {}

    def gain_sib():
        gain_copies[0] = remote(gain_one.at[0], gain_one.at[1], g_s.at[0], g_r.at[0], sib)

    def gain_across():
        gain_copies[0].wait_recv()
        gain_two[0] = gain_one[0] + gain_one[1]
        gain_copies[1] = remote(gain_two.at[0], gain_two.at[1], g_s.at[1], g_r.at[1], across)

    def gain_ring_start():
        gain_copies[1].wait_recv()
        gain_ring[0] = gain_two[0] + gain_two[1]
        gain_copies["up"] = remote(gain_ring.at[0], gain_ring.at[1], g_s.at[2], g_r.at[2], up)
        gain_copies["down"] = remote(gain_ring.at[0], gain_ring.at[7], g_s.at[3], g_r.at[3], down)

    def gain_ring_step(step):
        gain_copies["up"].wait_recv()
        gain_copies["down"].wait_recv()
        gain_copies["up"] = remote(
            gain_ring.at[step - 1], gain_ring.at[step], g_s.at[2 * step], g_r.at[2 * step], up
        )
        if step < 4:
            gain_copies["down"] = remote(
                gain_ring.at[9 - step], gain_ring.at[8 - step],
                g_s.at[2 * step + 1], g_r.at[2 * step + 1], down
            )

    def gain_finish():
        gain_copies["up"].wait_recv()
        z = me // 4
        total = gain_ring[lax.rem(z + 8, 8)]
        for a in range(1, 8):
            total += gain_ring[lax.rem(z - a + 8, 8)]
        gradient = jnp.sum(total, axis=0, keepdims=True)
        gain_part[0] = jnp.broadcast_to(gain[...] - learn_rate * gradient, (8, width))
        gain_copies["x"] = remote(gain_part.at[0], gain_part.at[1], g_s.at[9], g_r.at[9], partner)

    def gain_average():
        gain_copies["x"].wait_recv()
        gain_new[...] = 0.5 * (gain_part[0, 0:1, :] + gain_part[1, 0:1, :])
        write = pltpu.make_async_copy(gain_new, gain_out, out_sem.at[count + 1])
        write.start()
        writes.append(write)

    product(0)
    product(1)
    add_sib(0)
    product(2)
    add_sib(1)
    term(3)
    scatter_first()
    for i in range(3, count):
        product(i)
        add_sib(i - 1)
        if i == 5:
            scatter_step(3)
    add_sib(count - 1)
    extra = {
        1: [lambda: scatter_step(2)],
        3: [lambda: scatter_step(1)],
        5: [scatter_last, gain_sib],
        6: [gain_across],
        7: [gain_ring_start],
        8: [lambda: gain_ring_step(2)],
        9: [lambda: gain_ring_step(3)],
        10: [lambda: gain_ring_step(4)],
        11: [gain_finish],
    }
    for i in range(count):
        add_across(i)
        for action in extra.get(i, ()):
            action()
        if i >= 3:
            average(i - 3)
    for i in range(count - 3, count):
        average(i)
    gain_average()

    for copy in sent:
        copy.wait_send()
    for write in writes:
        write.wait()


def step_on_device(level, tokens, cotangent, gain, w_gate, w_up, w_down):
    rows, width = tokens.shape
    units = w_down.shape[0]
    count = 3 * (width // WIDTH)
    anywhere = pl.BlockSpec(memory_space=pl.ANY)
    dma = pltpu.SemaphoreType.DMA
    return pl.pallas_call(
        functools.partial(kernel, level),
        out_shape=(
            jax.ShapeDtypeStruct((rows, width), BF16),
            jax.ShapeDtypeStruct((1, width), F32),
            jax.ShapeDtypeStruct((units, width), F32),
            jax.ShapeDtypeStruct((units, width), F32),
            jax.ShapeDtypeStruct((units, width), F32),
        ),
        in_specs=[anywhere] * 6,
        out_specs=(anywhere,) * 5,
        scratch_shapes=[
            pltpu.VMEM((rows, width), BF16),
            pltpu.VMEM((1, width), F32),
            pltpu.VMEM((2, width, units), F32),
            pltpu.VMEM((3, units, width), F32),
            pltpu.VMEM((3, 4 * units, width), BF16),
            pltpu.VMEM((8, rows, width), BF16),
            pltpu.VMEM((8, rows, width), BF16),
            pltpu.VMEM((2, 4, 2 * rows, 4 * units), BF16),
            pltpu.VMEM((3, 4 * units, 8 * rows), BF16),
            pltpu.VMEM((8, rows, width), BF16),
            pltpu.VMEM((count, 2, units, WIDTH), BF16),
            pltpu.VMEM((count, 2, units, WIDTH), BF16),
            pltpu.VMEM((count, 2, units, WIDTH), F32),
            pltpu.VMEM((count, units, WIDTH), BF16),
            pltpu.VMEM((count, units, WIDTH), BF16),
            pltpu.VMEM((count, units, WIDTH), BF16),
            pltpu.VMEM((count, units, WIDTH), BF16),
            pltpu.VMEM((2, 3, rows, width), BF16),
            pltpu.VMEM((2, 4, rows, width), BF16),
            pltpu.VMEM((2, 8, width), F32),
            pltpu.VMEM((2, 8, width), F32),
            pltpu.VMEM((8, 8, width), F32),
            pltpu.VMEM((2, 8, width), F32),
            pltpu.VMEM((1, width), F32),
            pltpu.VMEM((rows, width), BF16),
            dma((6,)),
            dma((count + 2,)),
            dma((2, 2, 4)),
            dma((2, 2, 4)),
            dma((3, 3)),
            dma((3, 3)),
            dma((count,)),
            dma((count,)),
            dma((count,)),
            dma((count,)),
            dma((count,)),
            dma((count,)),
            dma((2, 4)),
            dma((2, 4)),
            dma((10,)),
            dma((10,)),
        ],
        compiler_params=pltpu.CompilerParams(
            collective_id=level, has_side_effects=True, vmem_limit_bytes=60 * 2**20
        ),
        cost_estimate=pl.CostEstimate(
            flops=8 * 2**30, bytes_accessed=8 * 2**20, transcendentals=2**18
        ),
    )(tokens, cotangent, gain, w_gate, w_up, w_down)


def local(tokens, cotangent, gain, w_gate, w_up, w_down, step_index):
    level_count = lax.axis_size("rep").bit_length() - 1
    branches = [functools.partial(step_on_device, level) for level in range(level_count)]
    input_grad, new_gain, gate_t, up_t, new_down = lax.switch(
        step_index[0] % level_count, branches,
        tokens[0], cotangent[0], gain, w_gate[0], w_up[0], w_down[0],
    )
    return (input_grad[None], new_gain, gate_t.T[None], up_t.T[None], new_down[None])


def solution(mesh):
    in_specs = (
        P("rep", "fsdp", None),
        P("rep", "fsdp", None),
        P("rep", None),
        P("rep", None, "fsdp"),
        P("rep", None, "fsdp"),
        P("rep", "fsdp", None),
        P(),
    )
    out_specs = (
        P("rep", "fsdp", None),
        P("rep", None),
        P("rep", None, "fsdp"),
        P("rep", None, "fsdp"),
        P("rep", "fsdp", None),
    )
    return jax.shard_map(local, mesh=mesh, in_specs=in_specs, out_specs=out_specs, check_vma=False)
```

```python
import functools

import jax
import jax.numpy as jnp
from jax import lax
from jax.experimental import pallas as pl
from jax.experimental.pallas import tpu as pltpu
from jax.sharding import PartitionSpec as P

MESH = pl.DeviceIdType.MESH
F32 = jnp.float32
BF16 = jnp.bfloat16

learn_rate = 0.02
epsilon = 1e-05

NT = (((1,), (1,)), ((), ()))
NN = (((1,), (0,)), ((), ()))

OWN, FOUR = 6, 7
DEPTH = 3
WIDTH = 512


def kernel(
    level,
    tok_hbm, cot_hbm, gain_hbm, wg_hbm, wu_hbm, wd_hbm,
    ig_out, gain_out, ng_out, nu_out, nd_out,
    tok, gain, raw, wt, wb, normed, cot, back, xt, terms,
    sib_out, sib_in, keep, y_out, y_in, x_out, x_in, rs_out, rs_in, slopes, turned,
    gain_one, gain_two, gain_ring, gain_part, gain_new, ig,
    in_sem, out_sem, ag_s, ag_r, w_s, w_r, sib_s, sib_r, y_s, y_r, x_s, x_r,
    rs_s, rs_r, g_s, g_r,
):
    rep = lax.axis_index("rep")
    me = lax.axis_index("fsdp")
    n_fsdp = lax.axis_size("fsdp")
    width = tok.shape[1]
    rows = tok.shape[0]
    units = wt.shape[1]
    pieces = width // WIDTH
    count = 3 * pieces
    in_scale = width ** (-0.5)
    out_scale = (units * n_fsdp) ** (-0.5)

    up = (rep, lax.rem(me + 4, n_fsdp))
    down = (rep, lax.rem(me + n_fsdp - 4, n_fsdp))
    sib = (rep, me + 1 - 2 * lax.rem(me, 2))
    across = (rep, me + 2 - 4 * lax.rem(me // 2, 2))
    far = 1 << level
    partner = (rep + far - 2 * far * lax.rem(rep // far, 2), me)
    ring = (up, down)

    def remote(src, dst, send, recv, device):
        return pltpu.make_async_remote_copy(
            src_ref=src, dst_ref=dst, send_sem=send, recv_sem=recv,
            device_id=device, device_id_type=MESH,
        )

    def at_tile(start, size):
        return pl.ds(pl.multiple_of(start, size), size)

    loads = [
        pltpu.make_async_copy(cot_hbm, cot.at[OWN], in_sem.at[0]),
        pltpu.make_async_copy(tok_hbm, tok, in_sem.at[1]),
        pltpu.make_async_copy(gain_hbm, gain, in_sem.at[2]),
        pltpu.make_async_copy(wg_hbm, raw.at[0], in_sem.at[3]),
        pltpu.make_async_copy(wu_hbm, raw.at[1], in_sem.at[4]),
        pltpu.make_async_copy(wd_hbm, wt.at[2], in_sem.at[5]),
    ]
    for load in loads:
        load.start()

    barrier = pltpu.get_barrier_semaphore()
    for other in (up, down, sib, across, partner):
        pl.semaphore_signal(barrier, inc=1, device_id=other, device_id_type=MESH)
    pl.semaphore_wait(barrier, 5)

    def gather(which, direction, step):
        buffer = (normed, cot)[which]
        first = 1 // step
        src = buffer.at[first * OWN + (1 - first) * (2 * (step - 2) + direction)]
        return remote(
            src, buffer.at[2 * (step - 1) + direction],
            ag_s.at[which, direction, step - 1], ag_r.at[which, direction, step - 1],
            ring[direction],
        )

    def gather_half(which, direction):
        buffer = (normed, cot)[which]
        part = pl.ds(direction * half, half)
        return remote(
            buffer.at[4 + direction, part], buffer.at[FOUR, part],
            ag_s.at[which, direction, 3], ag_r.at[which, direction, 3], ring[direction],
        )

    half = rows // 2
    loads[1].wait()
    loads[2].wait()

    @pl.loop(0, rows // 16)
    def _(r):
        part = at_tile(r * 16, 16)
        values = tok[part, :].astype(F32)
        inv_rms = lax.rsqrt(jnp.mean(values * values, axis=1, keepdims=True) + epsilon)
        normed[OWN, part, :] = ((values * inv_rms) * gain[...]).astype(BF16)

    for direction in (0, 1):
        gather(0, direction, 1).start()
    loads[0].wait()
    for direction in (0, 1):
        gather(1, direction, 1).start()

    def weight_across(m):
        return remote(
            wb.at[m, pl.ds(0, units)], wb.at[m, pl.ds(2 * units, units)],
            w_s.at[m, 0], w_r.at[m, 0], across,
        )

    def weight_sib(m):
        return remote(
            wb.at[m, pl.ds(0, units)], wb.at[m, pl.ds(units, units)],
            w_s.at[m, 1], w_r.at[m, 1], sib,
        )

    def weight_passed(m):
        return remote(
            wb.at[m, pl.ds(2 * units, units)], wb.at[m, pl.ds(3 * units, units)],
            w_s.at[m, 2], w_r.at[m, 2], sib,
        )

    for m in (0, 1):
        loads[3 + m].wait()

        @pl.loop(0, width // 128)
        def _(c):
            cols = at_tile(c * 128, 128)
            block = raw[m, cols, :].T
            wt[m, :, cols] = block
            wb[m, 0:units, cols] = block.astype(BF16)

        weight_across(m).start()
        weight_sib(m).start()
    loads[5].wait()

    @pl.loop(0, width // 128)
    def _(c):
        cols = at_tile(c * 128, 128)
        wb[2, 0:units, cols] = wt[2, :, cols].astype(BF16)

    weight_across(2).start()
    weight_sib(2).start()

    def tokens_of(buffer, g):
        return buffer[pl.ds(2 * g, 2)].reshape(2 * rows, width)

    def lanes_of(g):
        return at_tile(g * (2 * rows), 2 * rows)

    dot_nt = functools.partial(lax.dot_general, dimension_numbers=NT, preferred_element_type=F32)

    def forward(g, tile):
        cols = at_tile(tile * (2 * units), 2 * units)
        group = tokens_of(normed, g)
        gate_pre = dot_nt(group, wb[0, cols, :]) * in_scale
        up_pre = dot_nt(group, wb[1, cols, :]) * in_scale
        sigmoid_gate = jax.nn.sigmoid(gate_pre)
        activated = gate_pre * sigmoid_gate
        xt[2, cols, lanes_of(g)] = (activated * up_pre).T.astype(BF16)
        slopes[0, g, :, cols] = up_pre * sigmoid_gate * (1.0 + gate_pre * (1.0 - sigmoid_gate))
        slopes[1, g, :, cols] = activated

    def backward(g, tile):
        cols = at_tile(tile * (2 * units), 2 * units)
        grad_hidden = dot_nt(tokens_of(cot, g), wb[2, cols, :]) * out_scale
        for n in (0, 1):
            grad = grad_hidden * slopes[n, g, :, cols]
            back[n, g, :, cols] = grad.astype(BF16)
            xt[n, cols, lanes_of(g)] = grad.T.astype(BF16)

    def term(g):
        @pl.loop(0, pieces)
        def _(c):
            part = at_tile(c * WIDTH, WIDTH)
            value = lax.dot_general(back[0, g], wb[0, :, part], NN, preferred_element_type=F32)
            value += lax.dot_general(back[1, g], wb[1, :, part], NN, preferred_element_type=F32)
            value = value * in_scale
            terms[pl.ds(2 * g, 2), :, part] = value.astype(BF16).reshape(2, rows, WIDTH)
            along = value * normed[pl.ds(2 * g, 2), :, part].reshape(2 * rows, WIDTH).astype(F32)
            gain_one[0, :, part] += jnp.sum(along.reshape(rows // 4, 8, WIDTH), axis=0)

    gain_one[0] = jnp.zeros((8, width), F32)

    @pl.loop(0, 4)
    def _(i):
        step = i + 1

        @pl.when(i < 3)
        def _():
            for direction in (0, 1):
                gather(0, direction, step).wait_recv()

        @pl.when(i < 2)
        def _():
            for direction in (0, 1):
                gather(0, direction, step + 1).start()

        @pl.when(i == 2)
        def _():
            for direction in (0, 1):
                gather_half(0, direction).start()

        @pl.when(i == 3)
        def _():
            for direction in (0, 1):
                gather_half(0, direction).wait_recv()

        @pl.when(i == 0)
        def _():
            for m in range(3):
                weight_sib(m).wait_recv()

        forward(i, 0)

        @pl.when(i < 3)
        def _():
            for direction in (0, 1):
                gather(1, direction, step).wait_recv()

        @pl.when(i < 2)
        def _():
            for direction in (0, 1):
                gather(1, direction, step + 1).start()

        @pl.when(i == 2)
        def _():
            for direction in (0, 1):
                gather_half(1, direction).start()

        @pl.when(i < 3)
        def _():
            weight_across(i).wait_recv()
            weight_passed(i).start()
            backward(i, 0)

        @pl.when(i == 1)
        def _():
            for m in (0, 1):
                weight_passed(m).wait_recv()

        low = i - i * (1 - i // 2)
        high = i + 1 - 1 // (i + 1)

        @pl.loop(low, high)
        def _(g):
            forward(g, 1)

    for direction in (0, 1):
        gather_half(1, direction).wait_recv()

    def scatter_first(direction):
        part = pl.ds(direction * half, half)
        return remote(
            terms.at[FOUR, part], rs_in.at[direction, 0, part],
            rs_s.at[direction, 0], rs_r.at[direction, 0], ring[direction],
        )

    def scatter_send(direction, step):
        return remote(
            rs_out.at[direction, 3 - step], rs_in.at[direction, 4 - step],
            rs_s.at[direction, 4 - step], rs_r.at[direction, 4 - step], ring[direction],
        )

    def scatter_step(step):
        for direction in (0, 1):
            if step == 3:
                scatter_first(direction).wait_recv()
            else:
                scatter_send(direction, step + 1).wait_recv()
            slot = 2 * (step - 1) + 1 - direction

            @pl.loop(0, rows // 16)
            def _(r):
                part = at_tile(r * 16, 16)
                value = terms[slot, part, :].astype(F32)
                if step == 3:
                    inside = (r // (half // 16)) == direction
                    came = jnp.where(inside, rs_in[direction, 0, part, :].astype(F32), 0.0)
                else:
                    came = rs_in[direction, 3 - step, part, :].astype(F32)
                rs_out[direction, 3 - step, part, :] = (value + came).astype(BF16)

            scatter_send(direction, step).start()

    def scatter_last():
        for direction in (0, 1):
            scatter_send(direction, 1).wait_recv()
        @pl.loop(0, rows // 16)
        def _(r):
            part = at_tile(r * 16, 16)
            values = tok[part, :].astype(F32)
            inv_rms = lax.rsqrt(jnp.mean(values * values, axis=1, keepdims=True) + epsilon)
            unit = values * inv_rms
            grad = (
                terms[OWN, part, :].astype(F32)
                + rs_in[0, 3, part, :].astype(F32)
                + rs_in[1, 3, part, :].astype(F32)
            )
            scaled = grad * gain[...]
            mean = jnp.mean(scaled * unit, axis=1, keepdims=True)
            ig[part, :] = (
                cot[OWN, part, :].astype(F32) + inv_rms * (scaled - unit * mean)
            ).astype(BF16)

        ig_write().start()

    def ig_write():
        return pltpu.make_async_copy(ig, ig_out, out_sem.at[count])

    def gain_copy(name, step=1):
        if name == "sib":
            src, dst, sem, device = gain_one.at[0], gain_one.at[1], 0, sib
        elif name == "across":
            src, dst, sem, device = gain_two.at[0], gain_two.at[1], 1, across
        elif name == "partner":
            src, dst, sem, device = gain_part.at[0], gain_part.at[1], 9, partner
        elif name == "up":
            src, dst, sem, device = gain_ring.at[step - 1], gain_ring.at[step], 2 * step, up
        else:
            src, dst, sem, device = (
                gain_ring.at[(9 - step) % 8], gain_ring.at[8 - step], 2 * step + 1, down
            )
        return remote(src, dst, g_s.at[sem], g_r.at[sem], device)

    def gain_sib():
        gain_copy("sib").start()

    def gain_across():
        gain_copy("sib").wait_recv()
        gain_two[0] = gain_one[0] + gain_one[1]
        gain_copy("across").start()

    def gain_ring_start():
        gain_copy("across").wait_recv()
        gain_ring[0] = gain_two[0] + gain_two[1]
        gain_copy("up").start()
        gain_copy("down").start()

    def gain_ring_step(step):
        gain_copy("up", step - 1).wait_recv()
        gain_copy("down", step - 1).wait_recv()
        gain_copy("up", step).start()
        if step < 4:
            gain_copy("down", step).start()

    def gain_finish():
        gain_copy("up", 4).wait_recv()
        z = me // 4
        total = gain_ring[lax.rem(z + 8, 8)]
        for a in range(1, 8):
            total += gain_ring[lax.rem(z - a + 8, 8)]
        gradient = jnp.sum(total, axis=0, keepdims=True) / gain[...]
        gain_part[0] = jnp.broadcast_to(gain[...] - learn_rate * gradient, (8, width))
        gain_copy("partner").start()

    def gain_write():
        return pltpu.make_async_copy(gain_new, gain_out, out_sem.at[count + 1])

    def gain_average():
        gain_copy("partner").wait_recv()
        gain_new[...] = 0.5 * (gain_part[0, 0:1, :] + gain_part[1, 0:1, :])
        gain_write().start()

    def piece(i):
        block = i // pieces
        m = block + 2 - 3 * ((block + 2) // 3)
        return m, at_tile((i - block * pieces) * WIDTH, WIDTH)

    def sib_copy(i):
        return remote(sib_out.at[i], sib_in.at[i], sib_s.at[i], sib_r.at[i], sib)

    def y_copy(i):
        return remote(y_out.at[i], y_in.at[i], y_s.at[i], y_r.at[i], across)

    def x_copy(i):
        return remote(x_out.at[i], x_in.at[i], x_s.at[i], x_r.at[i], partner)

    def product(i, m, buffer, scale):
        _m, cols = piece(i)
        right = buffer[:, :, cols].reshape(8 * rows, WIDTH)
        for tile in (0, 1):
            part = slice(tile * 2 * units, (tile + 1) * 2 * units)
            value = lax.dot_general(xt[m, part, :], right, NN, preferred_element_type=F32)
            value = value * scale
            keep[i, tile] = value[:units]
            sib_out[i, tile] = value[units:].astype(BF16)
        sib_copy(i).start()

    def add_sib(i):
        sib_copy(i).wait_recv()
        y_out[i] = (keep[i, 1] + sib_in[i, 1].astype(F32)).astype(BF16)
        keep[i, 0] += sib_in[i, 0].astype(F32)

    def add_across(i):
        m, cols = piece(i)
        y_copy(i).wait_recv()
        new = wt[m, :, cols] - learn_rate * (keep[i, 0] + y_in[i].astype(F32))
        keep[i, 0] = new
        x_out[i] = new.astype(BF16)
        x_copy(i).start()

        @pl.when(i < count - DEPTH)
        def _():
            y_copy(i + DEPTH).start()

    def write(target, i):
        m, cols = piece(i)
        return pltpu.make_async_copy(keep.at[i, 0], target.at[:, cols], out_sem.at[i])

    def write_turned(target, i):
        m, cols = piece(i)
        return pltpu.make_async_copy(turned.at[i], target.at[cols], out_sem.at[i])

    def average(i):
        x_copy(i).wait_recv()
        keep[i, 0] = 0.5 * (keep[i, 0] + x_in[i].astype(F32))

        @pl.when(i < pieces)
        def _():
            write(nd_out, i).start()

        @pl.when(i >= pieces)
        def _():
            turned[i] = keep[i, 0].T

        @pl.when((i >= pieces) & (i < 2 * pieces))
        def _():
            write_turned(ng_out, i).start()

        @pl.when(i >= 2 * pieces)
        def _():
            write_turned(nu_out, i).start()

    @pl.loop(0, pieces)
    def _(i):
        product(i, 2, cot, out_scale)

    weight_passed(2).wait_recv()

    @pl.loop(0, 5)
    def _(j):
        last = 2 // (j + 1) - 1 // (j + 1)
        backward(3 * last + (j - 2) * (1 - last), 1 - 1 // (j + 1))

        @pl.when(j < pieces)
        def _():
            add_sib(j)

        @pl.when(j < DEPTH)
        def _():
            y_copy(j).start()

        @pl.when(j == 1)
        def _():
            term(3)
            for direction in (0, 1):
                scatter_first(direction).start()

    @pl.loop(pieces, count)
    def _(i):
        m, _cols = piece(i)
        product(i, m, normed, in_scale)

        @pl.when(i > pieces)
        def _():
            add_sib(i - 1)

        @pl.when(i < pieces + 3)
        def _():
            term(2 + pieces - i)

        @pl.when(i == pieces + 3)
        def _():
            scatter_step(3)
            gain_sib()

        for p, at in enumerate((pieces + 2, pieces + 5)):
            @pl.when(i == at)
            def _():
                add_across(p)

    add_sib(count - 1)

    extra = {
        2: gain_across,
        3: gain_ring_start,
        4: lambda: (scatter_step(2), gain_ring_step(2)),
        5: lambda: gain_ring_step(3),
        6: lambda: gain_ring_step(4),
        7: lambda: (scatter_step(1), gain_finish()),
        10: scatter_last,
    }

    @pl.loop(2, count + 2)
    def _(i):
        @pl.when(i < count)
        def _():
            add_across(i)

        for at, action in extra.items():
            @pl.when(i == at)
            def _():
                action()

        average(i - 2)

    gain_average()

    for which in (0, 1):
        for direction in (0, 1):
            for step in (1, 2, 3):
                gather(which, direction, step).wait_send()
            gather_half(which, direction).wait_send()
    for m in range(3):
        for copy in (weight_across, weight_sib, weight_passed):
            copy(m).wait_send()
    for direction in (0, 1):
        scatter_first(direction).wait_send()
        for step in (3, 2, 1):
            scatter_send(direction, step).wait_send()
    for name in ("sib", "across", "partner"):
        gain_copy(name).wait_send()
    for step in (1, 2, 3, 4):
        gain_copy("up", step).wait_send()
        if step < 4:
            gain_copy("down", step).wait_send()

    @pl.loop(0, count)
    def _(i):
        sib_copy(i).wait_send()
        y_copy(i).wait_send()
        x_copy(i).wait_send()
        write(nd_out, i).wait()

    ig_write().wait()
    gain_write().wait()


def step_on_device(level, tokens, cotangent, gain, w_gate, w_up, w_down):
    rows, width = tokens.shape
    units = w_down.shape[0]
    count = 3 * (width // WIDTH)
    anywhere = pl.BlockSpec(memory_space=pl.ANY)
    dma = pltpu.SemaphoreType.DMA
    return pl.pallas_call(
        functools.partial(kernel, level),
        out_shape=(
            jax.ShapeDtypeStruct((rows, width), BF16),
            jax.ShapeDtypeStruct((1, width), F32),
            jax.ShapeDtypeStruct((width, units), F32),
            jax.ShapeDtypeStruct((width, units), F32),
            jax.ShapeDtypeStruct((units, width), F32),
        ),
        in_specs=[anywhere] * 6,
        out_specs=(anywhere,) * 5,
        scratch_shapes=[
            pltpu.VMEM((rows, width), BF16),
            pltpu.VMEM((1, width), F32),
            pltpu.VMEM((2, width, units), F32),
            pltpu.VMEM((3, units, width), F32),
            pltpu.VMEM((3, 4 * units, width), BF16),
            pltpu.VMEM((8, rows, width), BF16),
            pltpu.VMEM((8, rows, width), BF16),
            pltpu.VMEM((2, 4, 2 * rows, 4 * units), BF16),
            pltpu.VMEM((3, 4 * units, 8 * rows), BF16),
            pltpu.VMEM((8, rows, width), BF16),
            pltpu.VMEM((count, 2, units, WIDTH), BF16),
            pltpu.VMEM((count, 2, units, WIDTH), BF16),
            pltpu.VMEM((count, 2, units, WIDTH), F32),
            pltpu.VMEM((count, units, WIDTH), BF16),
            pltpu.VMEM((count, units, WIDTH), BF16),
            pltpu.VMEM((count, units, WIDTH), BF16),
            pltpu.VMEM((count, units, WIDTH), BF16),
            pltpu.VMEM((2, 3, rows, width), BF16),
            pltpu.VMEM((2, 4, rows, width), BF16),
            pltpu.VMEM((2, 4, 2 * rows, 4 * units), F32),
            pltpu.VMEM((count, WIDTH, units), F32),
            pltpu.VMEM((2, 8, width), F32),
            pltpu.VMEM((2, 8, width), F32),
            pltpu.VMEM((8, 8, width), F32),
            pltpu.VMEM((2, 8, width), F32),
            pltpu.VMEM((1, width), F32),
            pltpu.VMEM((rows, width), BF16),
            dma((6,)),
            dma((count + 2,)),
            dma((2, 2, 4)),
            dma((2, 2, 4)),
            dma((3, 3)),
            dma((3, 3)),
            dma((count,)),
            dma((count,)),
            dma((count,)),
            dma((count,)),
            dma((count,)),
            dma((count,)),
            dma((2, 4)),
            dma((2, 4)),
            dma((10,)),
            dma((10,)),
        ],
        compiler_params=pltpu.CompilerParams(
            collective_id=level, has_side_effects=True, vmem_limit_bytes=60 * 2**20
        ),
        cost_estimate=pl.CostEstimate(
            flops=8 * 2**30, bytes_accessed=8 * 2**20, transcendentals=2**18
        ),
    )(tokens, cotangent, gain, w_gate, w_up, w_down)


def local(tokens, cotangent, gain, w_gate, w_up, w_down, step_index):
    level_count = lax.axis_size("rep").bit_length() - 1
    branches = [functools.partial(step_on_device, level) for level in range(level_count)]
    input_grad, new_gain, new_gate, new_up, new_down = lax.switch(
        step_index[0] % level_count, branches,
        tokens[0], cotangent[0], gain, w_gate[0], w_up[0], w_down[0],
    )
    results = place_results(
        input_grad[None], new_gain, new_gate[None], new_up[None], new_down[None]
    )
    return tuple(results)


def place_results(*arrays):
    def body(*refs):
        n = len(refs) // 2
        sems = refs[-1]
        copies = [pltpu.make_async_copy(refs[i], refs[n + i], sems.at[i]) for i in range(n)]
        for copy in copies:
            copy.start()
        for copy in copies:
            copy.wait()

    anywhere = pl.BlockSpec(memory_space=pl.ANY)
    return pl.pallas_call(
        body,
        out_shape=tuple(jax.ShapeDtypeStruct(a.shape, a.dtype) for a in arrays),
        in_specs=[anywhere] * len(arrays),
        out_specs=(anywhere,) * len(arrays),
        scratch_shapes=[pltpu.SemaphoreType.DMA((len(arrays),))],
    )(*arrays)


def solution(mesh):
    in_specs = (
        P("rep", "fsdp", None),
        P("rep", "fsdp", None),
        P("rep", None),
        P("rep", None, "fsdp"),
        P("rep", None, "fsdp"),
        P("rep", "fsdp", None),
        P(),
    )
    out_specs = (
        P("rep", "fsdp", None),
        P("rep", None),
        P("rep", None, "fsdp"),
        P("rep", None, "fsdp"),
        P("rep", "fsdp", None),
    )
    return jax.shard_map(local, mesh=mesh, in_specs=in_specs, out_specs=out_specs, check_vma=False)
```

```python
import functools

import jax
import jax.numpy as jnp
from jax import lax
from jax.experimental import pallas as pl
from jax.experimental.pallas import tpu as pltpu
from jax.sharding import PartitionSpec as P

MESH = pl.DeviceIdType.MESH
F32 = jnp.float32
BF16 = jnp.bfloat16

learn_rate = 0.02
epsilon = 1e-05

NT = (((1,), (1,)), ((), ()))
NN = (((1,), (0,)), ((), ()))

OWN, FOUR = 6, 7
DEPTH = 4
TILE = 512
WIDTH = 256


def kernel(
    level,
    tok_hbm, cot_hbm, gain_hbm, wg_hbm, wu_hbm, wd_hbm,
    ig_out, gain_out, ng_out, nu_out, nd_out,
    tok, gain, raw, wt, wb, normed, cot, back, xt, terms,
    sib_out, sib_in, keep, y_out, y_in, x_out, x_in, rs_out, rs_in, slopes, turned,
    gain_one, gain_two, gain_ring, gain_part, gain_new, ig,
    in_sem, out_sem, ag_s, ag_r, w_s, w_r, sib_s, sib_r, y_s, y_r, x_s, x_r,
    rs_s, rs_r, g_s, g_r,
):
    rep = lax.axis_index("rep")
    me = lax.axis_index("fsdp")
    n_fsdp = lax.axis_size("fsdp")
    width = tok.shape[1]
    rows = tok.shape[0]
    units = wt.shape[1]
    pieces = width // WIDTH
    count = 3 * pieces
    in_scale = width ** (-0.5)
    out_scale = (units * n_fsdp) ** (-0.5)

    up = (rep, lax.rem(me + 4, n_fsdp))
    down = (rep, lax.rem(me + n_fsdp - 4, n_fsdp))
    sib = (rep, me + 1 - 2 * lax.rem(me, 2))
    across = (rep, me + 2 - 4 * lax.rem(me // 2, 2))
    far = 1 << level
    partner = (rep + far - 2 * far * lax.rem(rep // far, 2), me)
    third = (partner[0], across[1])
    others = (up, down, sib, across, partner) + ((third,) if level == 0 else ())
    ring = (up, down)

    def remote(src, dst, send, recv, device):
        return pltpu.make_async_remote_copy(
            src_ref=src, dst_ref=dst, send_sem=send, recv_sem=recv,
            device_id=device, device_id_type=MESH,
        )

    def at_tile(start, size):
        return pl.ds(pl.multiple_of(start, size), size)

    loads = [
        pltpu.make_async_copy(cot_hbm, cot.at[OWN], in_sem.at[0]),
        pltpu.make_async_copy(tok_hbm, tok, in_sem.at[1]),
        pltpu.make_async_copy(gain_hbm, gain, in_sem.at[2]),
        pltpu.make_async_copy(wg_hbm, raw.at[0], in_sem.at[3]),
        pltpu.make_async_copy(wu_hbm, raw.at[1], in_sem.at[4]),
        pltpu.make_async_copy(wd_hbm, wt.at[2], in_sem.at[5]),
    ]
    for load in loads:
        load.start()

    barrier = pltpu.get_barrier_semaphore()
    for other in others:
        pl.semaphore_signal(barrier, inc=1, device_id=other, device_id_type=MESH)
    pl.semaphore_wait(barrier, len(others))

    def gather(which, direction, step):
        buffer = (normed, cot)[which]
        first = 1 // step
        src = buffer.at[first * OWN + (1 - first) * (2 * (step - 2) + direction)]
        return remote(
            src, buffer.at[2 * (step - 1) + direction],
            ag_s.at[which, direction, step - 1], ag_r.at[which, direction, step - 1],
            ring[direction],
        )

    def gather_half(which, direction):
        buffer = (normed, cot)[which]
        part = pl.ds(direction * half, half)
        return remote(
            buffer.at[4 + direction, part], buffer.at[FOUR, part],
            ag_s.at[which, direction, 3], ag_r.at[which, direction, 3], ring[direction],
        )

    half = rows // 2
    loads[1].wait()
    loads[2].wait()

    @pl.loop(0, rows // 16)
    def _(r):
        part = at_tile(r * 16, 16)
        values = tok[part, :].astype(F32)
        inv_rms = lax.rsqrt(jnp.mean(values * values, axis=1, keepdims=True) + epsilon)
        normed[OWN, part, :] = ((values * inv_rms) * gain[...]).astype(BF16)

    for direction in (0, 1):
        gather(0, direction, 1).start()
    loads[0].wait()
    for direction in (0, 1):
        gather(1, direction, 1).start()

    def weight_across(m):
        return remote(
            wb.at[m, pl.ds(0, units)], wb.at[m, pl.ds(2 * units, units)],
            w_s.at[m, 0], w_r.at[m, 0], across,
        )

    def weight_sib(m):
        return remote(
            wb.at[m, pl.ds(0, units)], wb.at[m, pl.ds(units, units)],
            w_s.at[m, 1], w_r.at[m, 1], sib,
        )

    def weight_passed(m):
        return remote(
            wb.at[m, pl.ds(2 * units, units)], wb.at[m, pl.ds(3 * units, units)],
            w_s.at[m, 2], w_r.at[m, 2], sib,
        )

    for m in (0, 1):
        loads[3 + m].wait()

        @pl.loop(0, width // 128)
        def _(c):
            cols = at_tile(c * 128, 128)
            block = raw[m, cols, :].T
            wt[m, :, cols] = block
            wb[m, 0:units, cols] = block.astype(BF16)

        weight_across(m).start()
        weight_sib(m).start()
    loads[5].wait()

    @pl.loop(0, width // 128)
    def _(c):
        cols = at_tile(c * 128, 128)
        wb[2, 0:units, cols] = wt[2, :, cols].astype(BF16)

    weight_across(2).start()
    weight_sib(2).start()

    def tokens_of(buffer, g):
        return buffer[pl.ds(2 * g, 2)].reshape(2 * rows, width)

    def lanes_of(g):
        return at_tile(g * (2 * rows), 2 * rows)

    dot_nt = functools.partial(lax.dot_general, dimension_numbers=NT, preferred_element_type=F32)

    def forward(g, tile):
        cols = at_tile(tile * (2 * units), 2 * units)
        group = tokens_of(normed, g)
        gate_pre = dot_nt(group, wb[0, cols, :]) * in_scale
        up_pre = dot_nt(group, wb[1, cols, :]) * in_scale
        sigmoid_gate = jax.nn.sigmoid(gate_pre)
        activated = gate_pre * sigmoid_gate
        xt[2, cols, lanes_of(g)] = (activated * up_pre).T.astype(BF16)
        slopes[0, g, :, cols] = up_pre * sigmoid_gate * (1.0 + gate_pre * (1.0 - sigmoid_gate))
        slopes[1, g, :, cols] = activated

    def backward(g, tile):
        cols = at_tile(tile * (2 * units), 2 * units)
        grad_hidden = dot_nt(tokens_of(cot, g), wb[2, cols, :]) * out_scale
        for n in (0, 1):
            grad = grad_hidden * slopes[n, g, :, cols]
            back[n, g, :, cols] = grad.astype(BF16)
            xt[n, cols, lanes_of(g)] = grad.T.astype(BF16)

    def term(g):
        @pl.loop(0, width // TILE)
        def _(c):
            part = at_tile(c * TILE, TILE)
            value = lax.dot_general(back[0, g], wb[0, :, part], NN, preferred_element_type=F32)
            value += lax.dot_general(back[1, g], wb[1, :, part], NN, preferred_element_type=F32)
            value = value * in_scale
            terms[pl.ds(2 * g, 2), :, part] = value.astype(BF16).reshape(2, rows, TILE)
            along = value * normed[pl.ds(2 * g, 2), :, part].reshape(2 * rows, TILE).astype(F32)
            gain_one[0, :, part] += jnp.sum(along.reshape(rows // 4, 8, TILE), axis=0)

    gain_one[0] = jnp.zeros((8, width), F32)

    @pl.loop(0, 4)
    def _(i):
        step = i + 1

        @pl.when(i < 3)
        def _():
            for direction in (0, 1):
                gather(0, direction, step).wait_recv()

        @pl.when(i < 2)
        def _():
            for direction in (0, 1):
                gather(0, direction, step + 1).start()

        @pl.when(i == 2)
        def _():
            for direction in (0, 1):
                gather_half(0, direction).start()

        @pl.when(i == 3)
        def _():
            for direction in (0, 1):
                gather_half(0, direction).wait_recv()

        @pl.when(i == 0)
        def _():
            for m in range(3):
                weight_sib(m).wait_recv()

        forward(i, 0)

        @pl.when(i < 3)
        def _():
            for direction in (0, 1):
                gather(1, direction, step).wait_recv()

        @pl.when(i < 2)
        def _():
            for direction in (0, 1):
                gather(1, direction, step + 1).start()

        @pl.when(i == 2)
        def _():
            for direction in (0, 1):
                gather_half(1, direction).start()

        @pl.when(i < 3)
        def _():
            weight_across(i).wait_recv()
            weight_passed(i).start()
            backward(i, 0)

        @pl.when(i == 1)
        def _():
            for m in (0, 1):
                weight_passed(m).wait_recv()

        low = i - i * (1 - i // 2)
        high = i + 1 - 1 // (i + 1)

        @pl.loop(low, high)
        def _(g):
            forward(g, 1)

    def scatter_send(direction, chain, step):
        part = pl.ds(((direction + chain) % 2) * half, half)
        slot = 2 * (step - 1) + 1 - direction
        if step == 4:
            src = terms.at[FOUR, part]
        elif step == 3 and chain == 1:
            src = terms.at[slot, part]
        else:
            src = rs_out.at[direction, 3 - step, part]
        return remote(
            src, rs_in.at[direction, 4 - step, part],
            rs_s.at[direction, chain, 4 - step], rs_r.at[direction, chain, 4 - step],
            ring[direction],
        )

    def scatter_step(chain, step):
        for direction in (0, 1):
            scatter_send(direction, chain, step + 1).wait_recv()
            slot = 2 * (step - 1) + 1 - direction
            start = ((direction + chain) % 2) * half
            for r in range(start, start + half, 16):
                part = slice(r, r + 16)
                value = terms[slot, part, :].astype(F32)
                came = rs_in[direction, 3 - step, part, :].astype(F32)
                rs_out[direction, 3 - step, part, :] = (value + came).astype(BF16)
            scatter_send(direction, chain, step).start()

    def scatter_last():
        for direction in (0, 1):
            for chain in (0, 1):
                scatter_send(direction, chain, 1).wait_recv()
        @pl.loop(0, rows // 16)
        def _(r):
            part = at_tile(r * 16, 16)
            values = tok[part, :].astype(F32)
            inv_rms = lax.rsqrt(jnp.mean(values * values, axis=1, keepdims=True) + epsilon)
            unit = values * inv_rms
            grad = (
                terms[OWN, part, :].astype(F32)
                + rs_in[0, 3, part, :].astype(F32)
                + rs_in[1, 3, part, :].astype(F32)
            )
            scaled = grad * gain[...]
            mean = jnp.mean(scaled * unit, axis=1, keepdims=True)
            ig[part, :] = (
                cot[OWN, part, :].astype(F32) + inv_rms * (scaled - unit * mean)
            ).astype(BF16)

        ig_write().start()

    def ig_write():
        return pltpu.make_async_copy(ig, ig_out, out_sem.at[count])

    def gain_copy(name, step=1):
        if name == "sib":
            src, dst, sem, device = gain_one.at[0], gain_one.at[1], 0, sib
        elif name == "across":
            src, dst, sem, device = gain_two.at[0], gain_two.at[1], 1, across
        elif name == "partner":
            src, dst, sem, device = gain_part.at[0], gain_part.at[1], 9, partner
        elif name == "up":
            src, dst, sem, device = gain_ring.at[step - 1], gain_ring.at[step], 2 * step, up
        else:
            src, dst, sem, device = (
                gain_ring.at[(9 - step) % 8], gain_ring.at[8 - step], 2 * step + 1, down
            )
        return remote(src, dst, g_s.at[sem], g_r.at[sem], device)

    def gain_sib():
        gain_copy("sib").start()

    def gain_across():
        gain_copy("sib").wait_recv()
        gain_two[0] = gain_one[0] + gain_one[1]
        gain_copy("across").start()

    def gain_ring_start():
        gain_copy("across").wait_recv()
        gain_ring[0] = gain_two[0] + gain_two[1]
        gain_copy("up").start()
        gain_copy("down").start()

    def gain_ring_step(step):
        gain_copy("up", step - 1).wait_recv()
        gain_copy("down", step - 1).wait_recv()
        gain_copy("up", step).start()
        if step < 4:
            gain_copy("down", step).start()

    def gain_finish():
        gain_copy("up", 4).wait_recv()
        z = me // 4
        total = gain_ring[lax.rem(z + 8, 8)]
        for a in range(1, 8):
            total += gain_ring[lax.rem(z - a + 8, 8)]
        gradient = jnp.sum(total, axis=0, keepdims=True) / gain[...]
        gain_part[0] = jnp.broadcast_to(gain[...] - learn_rate * gradient, (8, width))
        gain_copy("partner").start()

    def gain_write():
        return pltpu.make_async_copy(gain_new, gain_out, out_sem.at[count + 1])

    def gain_average():
        gain_copy("partner").wait_recv()
        gain_new[...] = 0.5 * (gain_part[0, 0:1, :] + gain_part[1, 0:1, :])
        gain_write().start()

    def piece(i):
        block = i // pieces
        m = block + 2 - 3 * ((block + 2) // 3)
        return m, at_tile((i - block * pieces) * WIDTH, WIDTH)

    def sib_copy(i):
        return remote(sib_out.at[i], sib_in.at[i], sib_s.at[i], sib_r.at[i], sib)

    def y_copies(i):
        if level > 0:
            return (remote(y_out.at[i], y_in.at[i], y_s.at[0, i], y_r.at[0, i], across),)
        side = lax.rem(rep, 2)
        return (
            remote(y_out.at[i, side], y_in.at[i, 0], y_s.at[0, i], y_r.at[0, i], across),
            remote(y_out.at[i, 1 - side], y_in.at[i, 1], y_s.at[1, i], y_r.at[1, i], third),
        )

    def y_start(i):
        for copy in y_copies(i):
            copy.start()

    def x_copy(i):
        return remote(x_out.at[i], x_in.at[i], x_s.at[i], x_r.at[i], partner)

    def product(i, m, buffer, scale):
        _m, cols = piece(i)
        right = buffer[:, :, cols].reshape(8 * rows, WIDTH)
        for tile in (0, 1):
            part = slice(tile * 2 * units, (tile + 1) * 2 * units)
            value = lax.dot_general(xt[m, part, :], right, NN, preferred_element_type=F32)
            value = value * scale
            keep[i, tile] = value[:units]
            sib_out[i, tile] = value[units:].astype(BF16)
        sib_copy(i).start()

    def add_sib(i):
        sib_copy(i).wait_recv()
        value = (keep[i, 1] + sib_in[i, 1].astype(F32)).astype(BF16)
        y_out[i, 0] = value[:, :WIDTH // 2]
        y_out[i, 1] = value[:, WIDTH // 2:]
        keep[i, 0] += sib_in[i, 0].astype(F32)

    def add_across(i):
        m, cols = piece(i)
        for copy in y_copies(i):
            copy.wait_recv()
        if level > 0:
            parts = [y_in[i, n].astype(F32) for n in (0, 1)]
        else:
            came = y_in[i, 0].astype(F32) + y_in[i, 1].astype(F32)
            side = lax.rem(rep, 2)
            parts = [jnp.where(side == n, came, 0.0) for n in (0, 1)]
        total = keep[i, 0] + jnp.concatenate(parts, axis=1)
        new = wt[m, :, cols] - learn_rate * total
        keep[i, 0] = new
        x_out[i] = new.astype(BF16)
        x_copy(i).start()

        @pl.when(i < count - DEPTH)
        def _():
            y_start(i + DEPTH)

    def write(target, i):
        m, cols = piece(i)
        return pltpu.make_async_copy(keep.at[i, 0], target.at[:, cols], out_sem.at[i])

    def write_turned(target, i):
        m, cols = piece(i)
        return pltpu.make_async_copy(turned.at[i], target.at[cols], out_sem.at[i])

    def average(i):
        x_copy(i).wait_recv()
        keep[i, 0] = 0.5 * (keep[i, 0] + x_in[i].astype(F32))

        @pl.when(i < pieces)
        def _():
            write(nd_out, i).start()

        @pl.when(i >= pieces)
        def _():
            turned[i] = keep[i, 0].T

        @pl.when((i >= pieces) & (i < 2 * pieces))
        def _():
            write_turned(ng_out, i).start()

        @pl.when(i >= 2 * pieces)
        def _():
            write_turned(nu_out, i).start()

    for direction in (0, 1):
        gather_half(1, direction).wait_recv()

    @pl.loop(0, pieces + 1)
    def _(i):
        @pl.when(i < pieces)
        def _():
            product(i, 2, cot, out_scale)

        @pl.when(i > 0)
        def _():
            add_sib(i - 1)

        @pl.when((i > 0) & (i <= DEPTH))
        def _():
            y_start(i - 1)

    weight_passed(2).wait_recv()

    @pl.loop(0, 5)
    def _(j):
        last = 2 // (j + 1) - 1 // (j + 1)
        g = 3 * last + (4 - j) * (1 - last)
        backward(g, 1 - 1 // (j + 1))

        @pl.when(j > 0)
        def _():
            term(g)

        @pl.when(j == 1)
        def _():
            for direction in (0, 1):
                scatter_send(direction, 0, 4).start()

        @pl.when(j == 2)
        def _():
            for direction in (0, 1):
                scatter_send(direction, 1, 3).start()

        @pl.when(j > 1)
        def _():
            add_across(j - 2)

    gain_sib()

    extra = {
        3: lambda: scatter_step(0, 3),
        4: gain_across,
        5: lambda: scatter_step(1, 2),
        7: lambda: scatter_step(0, 2),
        9: lambda: scatter_step(1, 1),
        10: gain_ring_start,
        11: lambda: scatter_step(0, 1),
        16: lambda: (scatter_last(), gain_ring_step(2)),
        18: lambda: gain_ring_step(3),
        20: lambda: gain_ring_step(4),
        22: gain_finish,
    }

    @pl.loop(3, count + 3)
    def _(i):
        @pl.when(i < count - DEPTH - 1)
        def _():
            m, _cols = piece(i + DEPTH + 1)
            product(i + DEPTH + 1, m, normed, in_scale)

        @pl.when((i > 3) & (i < count - DEPTH))
        def _():
            add_sib(i + DEPTH)

        @pl.when(i < count)
        def _():
            add_across(i)

        for at, action in extra.items():
            @pl.when(i == at)
            def _():
                action()

        average(i - 3)

    gain_average()

    for which in (0, 1):
        for direction in (0, 1):
            for step in (1, 2, 3):
                gather(which, direction, step).wait_send()
            gather_half(which, direction).wait_send()
    for m in range(3):
        for copy in (weight_across, weight_sib, weight_passed):
            copy(m).wait_send()
    for direction in (0, 1):
        for chain in (0, 1):
            for step in (4, 3, 2, 1)[chain:]:
                scatter_send(direction, chain, step).wait_send()
    for name in ("sib", "across", "partner"):
        gain_copy(name).wait_send()
    for step in (1, 2, 3, 4):
        gain_copy("up", step).wait_send()
        if step < 4:
            gain_copy("down", step).wait_send()

    @pl.loop(0, count)
    def _(i):
        sib_copy(i).wait_send()
        for copy in y_copies(i):
            copy.wait_send()
        x_copy(i).wait_send()
        write(nd_out, i).wait()

    ig_write().wait()
    gain_write().wait()


def step_on_device(level, tokens, cotangent, gain, w_gate, w_up, w_down):
    rows, width = tokens.shape
    units = w_down.shape[0]
    count = 3 * (width // WIDTH)
    anywhere = pl.BlockSpec(memory_space=pl.ANY)
    dma = pltpu.SemaphoreType.DMA
    return pl.pallas_call(
        functools.partial(kernel, level),
        out_shape=(
            jax.ShapeDtypeStruct((rows, width), BF16),
            jax.ShapeDtypeStruct((1, width), F32),
            jax.ShapeDtypeStruct((width, units), F32),
            jax.ShapeDtypeStruct((width, units), F32),
            jax.ShapeDtypeStruct((units, width), F32),
        ),
        in_specs=[anywhere] * 6,
        out_specs=(anywhere,) * 5,
        scratch_shapes=[
            pltpu.VMEM((rows, width), BF16),
            pltpu.VMEM((1, width), F32),
            pltpu.VMEM((2, width, units), F32),
            pltpu.VMEM((3, units, width), F32),
            pltpu.VMEM((3, 4 * units, width), BF16),
            pltpu.VMEM((8, rows, width), BF16),
            pltpu.VMEM((8, rows, width), BF16),
            pltpu.VMEM((2, 4, 2 * rows, 4 * units), BF16),
            pltpu.VMEM((3, 4 * units, 8 * rows), BF16),
            pltpu.VMEM((8, rows, width), BF16),
            pltpu.VMEM((count, 2, units, WIDTH), BF16),
            pltpu.VMEM((count, 2, units, WIDTH), BF16),
            pltpu.VMEM((count, 2, units, WIDTH), F32),
            pltpu.VMEM((count, 2, units, WIDTH // 2), BF16),
            pltpu.VMEM((count, 2, units, WIDTH // 2), BF16),
            pltpu.VMEM((count, units, WIDTH), BF16),
            pltpu.VMEM((count, units, WIDTH), BF16),
            pltpu.VMEM((2, 3, rows, width), BF16),
            pltpu.VMEM((2, 4, rows, width), BF16),
            pltpu.VMEM((2, 4, 2 * rows, 4 * units), F32),
            pltpu.VMEM((count, WIDTH, units), F32),
            pltpu.VMEM((2, 8, width), F32),
            pltpu.VMEM((2, 8, width), F32),
            pltpu.VMEM((8, 8, width), F32),
            pltpu.VMEM((2, 8, width), F32),
            pltpu.VMEM((1, width), F32),
            pltpu.VMEM((rows, width), BF16),
            dma((6,)),
            dma((count + 2,)),
            dma((2, 2, 4)),
            dma((2, 2, 4)),
            dma((3, 3)),
            dma((3, 3)),
            dma((count,)),
            dma((count,)),
            dma((2, count)),
            dma((2, count)),
            dma((count,)),
            dma((count,)),
            dma((2, 2, 4)),
            dma((2, 2, 4)),
            dma((10,)),
            dma((10,)),
        ],
        compiler_params=pltpu.CompilerParams(
            collective_id=level, has_side_effects=True, vmem_limit_bytes=60 * 2**20
        ),
        cost_estimate=pl.CostEstimate(
            flops=8 * 2**30, bytes_accessed=8 * 2**20, transcendentals=2**18
        ),
    )(tokens, cotangent, gain, w_gate, w_up, w_down)


def local(tokens, cotangent, gain, w_gate, w_up, w_down, step_index):
    level_count = lax.axis_size("rep").bit_length() - 1
    branches = [functools.partial(step_on_device, level) for level in range(level_count)]
    input_grad, new_gain, new_gate, new_up, new_down = lax.switch(
        step_index[0] % level_count, branches,
        tokens[0], cotangent[0], gain, w_gate[0], w_up[0], w_down[0],
    )
    results = place_results(
        input_grad[None], new_gain, new_gate[None], new_up[None], new_down[None]
    )
    return tuple(results)


def place_results(*arrays):
    def body(*refs):
        n = len(refs) // 2
        sems = refs[-1]
        copies = [pltpu.make_async_copy(refs[i], refs[n + i], sems.at[i]) for i in range(n)]
        for copy in copies:
            copy.start()
        for copy in copies:
            copy.wait()

    anywhere = pl.BlockSpec(memory_space=pl.ANY)
    return pl.pallas_call(
        body,
        out_shape=tuple(jax.ShapeDtypeStruct(a.shape, a.dtype) for a in arrays),
        in_specs=[anywhere] * len(arrays),
        out_specs=(anywhere,) * len(arrays),
        scratch_shapes=[pltpu.SemaphoreType.DMA((len(arrays),))],
    )(*arrays)


def solution(mesh):
    in_specs = (
        P("rep", "fsdp", None),
        P("rep", "fsdp", None),
        P("rep", None),
        P("rep", None, "fsdp"),
        P("rep", None, "fsdp"),
        P("rep", "fsdp", None),
        P(),
    )
    out_specs = (
        P("rep", "fsdp", None),
        P("rep", None),
        P("rep", None, "fsdp"),
        P("rep", None, "fsdp"),
        P("rep", "fsdp", None),
    )
    return jax.shard_map(local, mesh=mesh, in_specs=in_specs, out_specs=out_specs, check_vma=False)
```

```python
import functools

import jax
import jax.numpy as jnp
from jax import lax
from jax.experimental import pallas as pl
from jax.experimental.pallas import tpu as pltpu
from jax.sharding import PartitionSpec as P

MESH = pl.DeviceIdType.MESH
F32 = jnp.float32
BF16 = jnp.bfloat16

learn_rate = 0.02
epsilon = 1e-05

NT = (((1,), (1,)), ((), ()))
NN = (((1,), (0,)), ((), ()))

OWN, FOUR = 6, 7
DEPTH = 5
TILE = 512
WIDTH = 256


def kernel(
    level,
    tok_hbm, cot_hbm, gain_hbm, wg_hbm, wu_hbm, wd_hbm,
    ig_out, gain_out, ng_out, nu_out, nd_out,
    tok, gain, raw, wt, wb, normed, cot, back, xt, terms,
    sib_out, sib_in, keep, y_out, y_in, x_out, x_in, rs_out, rs_in, slopes, turned,
    gain_one, gain_two, gain_ring, gain_part, gain_new, ig,
    in_sem, out_sem, ag_s, ag_r, w_s, w_r, sib_s, sib_r, y_s, y_r, x_s, x_r,
    rs_s, rs_r, g_s, g_r,
):
    rep = lax.axis_index("rep")
    me = lax.axis_index("fsdp")
    n_fsdp = lax.axis_size("fsdp")
    width = tok.shape[1]
    rows = tok.shape[0]
    units = wt.shape[1]
    pieces = width // WIDTH
    count = 3 * pieces
    in_scale = width ** (-0.5)
    out_scale = (units * n_fsdp) ** (-0.5)

    up = (rep, lax.rem(me + 4, n_fsdp))
    down = (rep, lax.rem(me + n_fsdp - 4, n_fsdp))
    sib = (rep, me + 1 - 2 * lax.rem(me, 2))
    across = (rep, me + 2 - 4 * lax.rem(me // 2, 2))
    far = 1 << level
    partner = (rep + far - 2 * far * lax.rem(rep // far, 2), me)
    third = (partner[0], across[1])
    others = (up, down, sib, across, partner) + ((third,) if level == 0 else ())
    ring = (up, down)

    def remote(src, dst, send, recv, device):
        return pltpu.make_async_remote_copy(
            src_ref=src, dst_ref=dst, send_sem=send, recv_sem=recv,
            device_id=device, device_id_type=MESH,
        )

    def at_tile(start, size):
        return pl.ds(pl.multiple_of(start, size), size)

    barrier = pltpu.get_barrier_semaphore()
    for other in others:
        pl.semaphore_signal(barrier, inc=1, device_id=other, device_id_type=MESH)
    loads = [
        pltpu.make_async_copy(cot_hbm, cot.at[OWN], in_sem.at[0]),
        pltpu.make_async_copy(tok_hbm, tok, in_sem.at[1]),
        pltpu.make_async_copy(gain_hbm, gain, in_sem.at[2]),
        pltpu.make_async_copy(wg_hbm, raw.at[0], in_sem.at[3]),
        pltpu.make_async_copy(wu_hbm, raw.at[1], in_sem.at[4]),
        pltpu.make_async_copy(wd_hbm, wt.at[2], in_sem.at[5]),
    ]
    for load in loads:
        load.start()

    pl.semaphore_wait(barrier, len(others))

    def gather(which, direction, step):
        buffer = (normed, cot)[which]
        first = 1 // step
        src = buffer.at[first * OWN + (1 - first) * (2 * (step - 2) + direction)]
        return remote(
            src, buffer.at[2 * (step - 1) + direction],
            ag_s.at[which, direction, step - 1], ag_r.at[which, direction, step - 1],
            ring[direction],
        )

    def gather_half(which, direction):
        buffer = (normed, cot)[which]
        part = pl.ds(direction * half, half)
        return remote(
            buffer.at[4 + direction, part], buffer.at[FOUR, part],
            ag_s.at[which, direction, 3], ag_r.at[which, direction, 3], ring[direction],
        )

    half = rows // 2
    loads[1].wait()
    loads[2].wait()

    @pl.loop(0, rows // 16)
    def _(r):
        part = at_tile(r * 16, 16)
        values = tok[part, :].astype(F32)
        inv_rms = lax.rsqrt(jnp.mean(values * values, axis=1, keepdims=True) + epsilon)
        normed[OWN, part, :] = ((values * inv_rms) * gain[...]).astype(BF16)

    for direction in (0, 1):
        gather(0, direction, 1).start()
    loads[0].wait()
    for direction in (0, 1):
        gather(1, direction, 1).start()

    def weight_across(m):
        return remote(
            wb.at[m, pl.ds(0, units)], wb.at[m, pl.ds(2 * units, units)],
            w_s.at[m, 0], w_r.at[m, 0], across,
        )

    def weight_sib(m):
        return remote(
            wb.at[m, pl.ds(0, units)], wb.at[m, pl.ds(units, units)],
            w_s.at[m, 1], w_r.at[m, 1], sib,
        )

    def weight_passed(m):
        return remote(
            wb.at[m, pl.ds(2 * units, units)], wb.at[m, pl.ds(3 * units, units)],
            w_s.at[m, 2], w_r.at[m, 2], sib,
        )

    for m in (0, 1):
        loads[3 + m].wait()

        @pl.loop(0, width // 128)
        def _(c):
            cols = at_tile(c * 128, 128)
            block = raw[m, cols, :].T
            wt[m, :, cols] = block
            wb[m, 0:units, cols] = block.astype(BF16)

        weight_across(m).start()
        weight_sib(m).start()
    loads[5].wait()

    @pl.loop(0, width // 128)
    def _(c):
        cols = at_tile(c * 128, 128)
        wb[2, 0:units, cols] = wt[2, :, cols].astype(BF16)

    weight_across(2).start()
    weight_sib(2).start()

    def tokens_of(buffer, g):
        return buffer[pl.ds(2 * g, 2)].reshape(2 * rows, width)

    def lanes_of(g):
        return at_tile(g * (2 * rows), 2 * rows)

    dot_nt = functools.partial(lax.dot_general, dimension_numbers=NT, preferred_element_type=F32)

    def forward(g, tile):
        cols = at_tile(tile * (2 * units), 2 * units)
        group = tokens_of(normed, g)
        gate_pre = dot_nt(group, wb[0, cols, :]) * in_scale
        up_pre = dot_nt(group, wb[1, cols, :]) * in_scale
        sigmoid_gate = jax.nn.sigmoid(gate_pre)
        activated = gate_pre * sigmoid_gate
        xt[2, cols, lanes_of(g)] = (activated * up_pre).T.astype(BF16)
        slopes[0, g, :, cols] = up_pre * sigmoid_gate * (1.0 + gate_pre * (1.0 - sigmoid_gate))
        slopes[1, g, :, cols] = activated

    def backward(g, tile):
        cols = at_tile(tile * (2 * units), 2 * units)
        grad_hidden = dot_nt(tokens_of(cot, g), wb[2, cols, :]) * out_scale
        for n in (0, 1):
            grad = grad_hidden * slopes[n, g, :, cols]
            back[n, g, :, cols] = grad.astype(BF16)
            xt[n, cols, lanes_of(g)] = grad.T.astype(BF16)

    def term(g):
        @pl.loop(0, width // TILE)
        def _(c):
            part = at_tile(c * TILE, TILE)
            value = lax.dot_general(back[0, g], wb[0, :, part], NN, preferred_element_type=F32)
            value += lax.dot_general(back[1, g], wb[1, :, part], NN, preferred_element_type=F32)
            value = value * in_scale
            terms[pl.ds(2 * g, 2), :, part] = value.astype(BF16).reshape(2, rows, TILE)
            along = value * normed[pl.ds(2 * g, 2), :, part].reshape(2 * rows, TILE).astype(F32)
            gain_one[0, :, part] += jnp.sum(along, axis=0, keepdims=True)

    gain_one[0] = jnp.zeros((1, width), F32)

    @pl.loop(0, 4)
    def _(i):
        step = i + 1

        @pl.when(i < 3)
        def _():
            for direction in (0, 1):
                gather(0, direction, step).wait_recv()

        @pl.when(i < 2)
        def _():
            for direction in (0, 1):
                gather(0, direction, step + 1).start()

        @pl.when(i == 2)
        def _():
            for direction in (0, 1):
                gather_half(0, direction).start()

        @pl.when(i == 3)
        def _():
            for direction in (0, 1):
                gather_half(0, direction).wait_recv()

        @pl.when(i == 0)
        def _():
            for m in range(3):
                weight_sib(m).wait_recv()

        forward(i, 0)

        @pl.when(i < 3)
        def _():
            for direction in (0, 1):
                gather(1, direction, step).wait_recv()

        @pl.when(i < 2)
        def _():
            for direction in (0, 1):
                gather(1, direction, step + 1).start()

        @pl.when(i == 2)
        def _():
            for direction in (0, 1):
                gather_half(1, direction).start()

        @pl.when(i < 3)
        def _():
            weight_across(i).wait_recv()
            weight_passed(i).start()
            backward(i, 0)

        @pl.when(i == 1)
        def _():
            for m in (0, 1):
                weight_passed(m).wait_recv()

        low = i - i * (1 - i // 2)
        high = i + 1 - 1 // (i + 1)

        @pl.loop(low, high)
        def _(g):
            forward(g, 1)

    def scatter_send(direction, chain, step):
        part = pl.ds(((direction + chain) % 2) * half, half)
        slot = 2 * (step - 1) + 1 - direction
        if step == 4:
            src = terms.at[FOUR, part]
        elif step == 3 and chain == 1:
            src = terms.at[slot, part]
        else:
            src = rs_out.at[direction, 3 - step, part]
        return remote(
            src, rs_in.at[direction, 4 - step, part],
            rs_s.at[direction, chain, 4 - step], rs_r.at[direction, chain, 4 - step],
            ring[direction],
        )

    def scatter_step(chain, step):
        for direction in (0, 1):
            scatter_send(direction, chain, step + 1).wait_recv()
            slot = 2 * (step - 1) + 1 - direction
            start = ((direction + chain) % 2) * half
            for r in range(start, start + half, 16):
                part = slice(r, r + 16)
                value = terms[slot, part, :].astype(F32)
                came = rs_in[direction, 3 - step, part, :].astype(F32)
                rs_out[direction, 3 - step, part, :] = (value + came).astype(BF16)
            scatter_send(direction, chain, step).start()

    def scatter_last():
        for direction in (0, 1):
            for chain in (0, 1):
                scatter_send(direction, chain, 1).wait_recv()
        @pl.loop(0, rows // 16)
        def _(r):
            part = at_tile(r * 16, 16)
            values = tok[part, :].astype(F32)
            inv_rms = lax.rsqrt(jnp.mean(values * values, axis=1, keepdims=True) + epsilon)
            unit = values * inv_rms
            grad = (
                terms[OWN, part, :].astype(F32)
                + rs_in[0, 3, part, :].astype(F32)
                + rs_in[1, 3, part, :].astype(F32)
            )
            scaled = grad * gain[...]
            mean = jnp.mean(scaled * unit, axis=1, keepdims=True)
            ig[part, :] = (
                cot[OWN, part, :].astype(F32) + inv_rms * (scaled - unit * mean)
            ).astype(BF16)

        ig_write().start()

    def ig_write():
        return pltpu.make_async_copy(ig, ig_out, out_sem.at[count])

    def gain_copy(name, step=1):
        if name == "sib":
            src, dst, sem, device = gain_one.at[0], gain_one.at[1], 0, sib
        elif name == "across":
            src, dst, sem, device = gain_two.at[0], gain_two.at[1], 1, across
        elif name == "partner":
            src, dst, sem, device = gain_part.at[0], gain_part.at[1], 9, partner
        elif name == "up":
            src, dst, sem, device = gain_ring.at[step - 1], gain_ring.at[step], 2 * step, up
        else:
            src, dst, sem, device = (
                gain_ring.at[(9 - step) % 8], gain_ring.at[8 - step], 2 * step + 1, down
            )
        return remote(src, dst, g_s.at[sem], g_r.at[sem], device)

    def gain_sib():
        gain_one[0] = 0.5 * (
            gain[...] * (1.0 / n_fsdp) - learn_rate * (gain_one[0] / gain[...])
        )
        gain_copy("sib").start()

    def gain_partner():
        gain_copy("sib").wait_recv()
        gain_part[0] = gain_one[0] + gain_one[1]
        gain_copy("partner").start()

    def gain_across():
        gain_copy("partner").wait_recv()
        gain_two[0] = gain_part[0] + gain_part[1]
        gain_copy("across").start()

    def gain_ring_start():
        gain_copy("across").wait_recv()
        gain_ring[0] = gain_two[0] + gain_two[1]
        gain_copy("up").start()
        gain_copy("down").start()

    def gain_ring_step(step):
        gain_copy("up", step - 1).wait_recv()
        gain_copy("down", step - 1).wait_recv()
        gain_copy("up", step).start()
        if step < 4:
            gain_copy("down", step).start()

    def gain_finish():
        gain_copy("up", 4).wait_recv()
        z = me // 4
        total = gain_ring[lax.rem(z + 8, 8)]
        for a in range(1, 8):
            total += gain_ring[lax.rem(z - a + 8, 8)]
        gain_new[...] = total
        gain_write().start()

    def gain_write():
        return pltpu.make_async_copy(gain_new, gain_out, out_sem.at[count + 1])

    def piece(i):
        block = i // pieces
        m = block + 2 - 3 * ((block + 2) // 3)
        return m, at_tile((i - block * pieces) * WIDTH, WIDTH)

    def sib_copy(i):
        return remote(sib_out.at[i], sib_in.at[i], sib_s.at[i], sib_r.at[i], sib)

    def y_copies(i):
        if level > 0:
            return (remote(y_out.at[i], y_in.at[i], y_s.at[0, i], y_r.at[0, i], across),)
        side = lax.rem(rep, 2)
        return (
            remote(y_out.at[i, side], y_in.at[i, 0], y_s.at[0, i], y_r.at[0, i], across),
            remote(y_out.at[i, 1 - side], y_in.at[i, 1], y_s.at[1, i], y_r.at[1, i], third),
        )

    def y_start(i):
        for copy in y_copies(i):
            copy.start()

    def x_copy(i):
        return remote(x_out.at[i], x_in.at[i], x_s.at[i], x_r.at[i], partner)

    def product(i, m, buffer, scale):
        _m, cols = piece(i)
        right = buffer[:, :, cols].reshape(8 * rows, WIDTH)
        for tile in (0, 1):
            part = slice(tile * 2 * units, (tile + 1) * 2 * units)
            value = lax.dot_general(xt[m, part, :], right, NN, preferred_element_type=F32)
            value = value * scale
            keep[i, tile] = value[:units]
            sib_out[i, tile] = value[units:].astype(BF16)
        sib_copy(i).start()

    def add_sib(i):
        sib_copy(i).wait_recv()
        value = (keep[i, 1] + sib_in[i, 1].astype(F32)).astype(BF16)
        y_out[i, 0] = value[:, :WIDTH // 2]
        y_out[i, 1] = value[:, WIDTH // 2:]
        keep[i, 0] += sib_in[i, 0].astype(F32)

    def add_across(i):
        m, cols = piece(i)
        for copy in y_copies(i):
            copy.wait_recv()
        if level > 0:
            parts = [y_in[i, n].astype(F32) for n in (0, 1)]
        else:
            came = y_in[i, 0].astype(F32) + y_in[i, 1].astype(F32)
            side = lax.rem(rep, 2)
            parts = [jnp.where(side == n, came, 0.0) for n in (0, 1)]
        total = keep[i, 0] + jnp.concatenate(parts, axis=1)
        new = wt[m, :, cols] - learn_rate * total
        keep[i, 0] = new
        x_out[i] = new.astype(BF16)
        x_copy(i).start()

        @pl.when(i < count - DEPTH)
        def _():
            y_start(i + DEPTH)

    def write(target, i):
        m, cols = piece(i)
        return pltpu.make_async_copy(keep.at[i, 0], target.at[:, cols], out_sem.at[i])

    def write_turned(target, i):
        m, cols = piece(i)
        return pltpu.make_async_copy(turned.at[i], target.at[cols], out_sem.at[i])

    def average(i):
        x_copy(i).wait_recv()
        keep[i, 0] = 0.5 * (keep[i, 0] + x_in[i].astype(F32))

        @pl.when(i < pieces)
        def _():
            write(nd_out, i).start()

        @pl.when(i >= pieces)
        def _():
            turned[i] = keep[i, 0].T

        @pl.when((i >= pieces) & (i < 2 * pieces))
        def _():
            write_turned(ng_out, i).start()

        @pl.when(i >= 2 * pieces)
        def _():
            write_turned(nu_out, i).start()

    for direction in (0, 1):
        gather_half(1, direction).wait_recv()

    @pl.loop(0, pieces + 1)
    def _(i):
        @pl.when(i < pieces)
        def _():
            product(i, 2, cot, out_scale)

        @pl.when(i > 0)
        def _():
            add_sib(i - 1)

        @pl.when((i > 0) & (i <= DEPTH))
        def _():
            y_start(i - 1)

    weight_passed(2).wait_recv()

    @pl.loop(0, 5)
    def _(j):
        last = 2 // (j + 1) - 1 // (j + 1)
        backward(3 * last + (4 - j) * (1 - last), 1 - 1 // (j + 1))

    def start_chain(chain):
        for direction in (0, 1):
            scatter_send(direction, chain, 4 - chain).start()

    extra = {
        1: lambda: start_chain(0),
        2: lambda: start_chain(1),
        4: gain_sib,
        6: lambda: (scatter_step(0, 3), gain_partner()),
        8: lambda: scatter_step(1, 2),
        9: gain_across,
        10: lambda: scatter_step(0, 2),
        12: lambda: scatter_step(1, 1),
        14: lambda: (scatter_step(0, 1), gain_ring_start()),
        17: lambda: gain_ring_step(2),
        18: scatter_last,
        19: lambda: gain_ring_step(3),
        21: lambda: gain_ring_step(4),
        23: gain_finish,
    }

    @pl.loop(0, count + 3)
    def _(i):
        @pl.when(i < count - pieces)
        def _():
            m, _cols = piece(i + pieces)
            product(i + pieces, m, normed, in_scale)

        @pl.when((i > 0) & (i < count - pieces + 1))
        def _():
            add_sib(i + pieces - 1)

        @pl.when(i < count)
        def _():
            add_across(i)

        @pl.when((i > 0) & (i < 5))
        def _():
            term(4 - i)

        for at, action in extra.items():
            @pl.when(i == at)
            def _():
                action()

        @pl.when(i >= 3)
        def _():
            average(i - 3)

    for which in (0, 1):
        for direction in (0, 1):
            for step in (1, 2, 3):
                gather(which, direction, step).wait_send()
            gather_half(which, direction).wait_send()
    for m in range(3):
        for copy in (weight_across, weight_sib, weight_passed):
            copy(m).wait_send()
    for direction in (0, 1):
        for chain in (0, 1):
            for step in (4, 3, 2, 1)[chain:]:
                scatter_send(direction, chain, step).wait_send()
    for name in ("sib", "across", "partner"):
        gain_copy(name).wait_send()
    for step in (1, 2, 3, 4):
        gain_copy("up", step).wait_send()
        if step < 4:
            gain_copy("down", step).wait_send()

    @pl.loop(0, count)
    def _(i):
        sib_copy(i).wait_send()
        for copy in y_copies(i):
            copy.wait_send()
        x_copy(i).wait_send()
        write(nd_out, i).wait()

    ig_write().wait()
    gain_write().wait()


def step_on_device(level, tokens, cotangent, gain, w_gate, w_up, w_down):
    rows, width = tokens.shape
    units = w_down.shape[0]
    count = 3 * (width // WIDTH)
    anywhere = pl.BlockSpec(memory_space=pl.ANY)
    dma = pltpu.SemaphoreType.DMA
    return pl.pallas_call(
        functools.partial(kernel, level),
        out_shape=(
            jax.ShapeDtypeStruct((rows, width), BF16),
            jax.ShapeDtypeStruct((1, width), F32),
            jax.ShapeDtypeStruct((width, units), F32),
            jax.ShapeDtypeStruct((width, units), F32),
            jax.ShapeDtypeStruct((units, width), F32),
        ),
        in_specs=[anywhere] * 6,
        out_specs=(anywhere,) * 5,
        scratch_shapes=[
            pltpu.VMEM((rows, width), BF16),
            pltpu.VMEM((1, width), F32),
            pltpu.VMEM((2, width, units), F32),
            pltpu.VMEM((3, units, width), F32),
            pltpu.VMEM((3, 4 * units, width), BF16),
            pltpu.VMEM((8, rows, width), BF16),
            pltpu.VMEM((8, rows, width), BF16),
            pltpu.VMEM((2, 4, 2 * rows, 4 * units), BF16),
            pltpu.VMEM((3, 4 * units, 8 * rows), BF16),
            pltpu.VMEM((8, rows, width), BF16),
            pltpu.VMEM((count, 2, units, WIDTH), BF16),
            pltpu.VMEM((count, 2, units, WIDTH), BF16),
            pltpu.VMEM((count, 2, units, WIDTH), F32),
            pltpu.VMEM((count, 2, units, WIDTH // 2), BF16),
            pltpu.VMEM((count, 2, units, WIDTH // 2), BF16),
            pltpu.VMEM((count, units, WIDTH), BF16),
            pltpu.VMEM((count, units, WIDTH), BF16),
            pltpu.VMEM((2, 3, rows, width), BF16),
            pltpu.VMEM((2, 4, rows, width), BF16),
            pltpu.VMEM((2, 4, 2 * rows, 4 * units), F32),
            pltpu.VMEM((count, WIDTH, units), F32),
            pltpu.VMEM((2, 1, width), F32),
            pltpu.VMEM((2, 1, width), F32),
            pltpu.VMEM((8, 1, width), F32),
            pltpu.VMEM((2, 1, width), F32),
            pltpu.VMEM((1, width), F32),
            pltpu.VMEM((rows, width), BF16),
            dma((6,)),
            dma((count + 2,)),
            dma((2, 2, 4)),
            dma((2, 2, 4)),
            dma((3, 3)),
            dma((3, 3)),
            dma((count,)),
            dma((count,)),
            dma((2, count)),
            dma((2, count)),
            dma((count,)),
            dma((count,)),
            dma((2, 2, 4)),
            dma((2, 2, 4)),
            dma((10,)),
            dma((10,)),
        ],
        compiler_params=pltpu.CompilerParams(
            collective_id=level, has_side_effects=True, vmem_limit_bytes=60 * 2**20
        ),
        cost_estimate=pl.CostEstimate(
            flops=8 * 2**30, bytes_accessed=8 * 2**20, transcendentals=2**18
        ),
    )(tokens, cotangent, gain, w_gate, w_up, w_down)


def local(tokens, cotangent, gain, w_gate, w_up, w_down, step_index):
    level_count = lax.axis_size("rep").bit_length() - 1
    branches = [functools.partial(step_on_device, level) for level in range(level_count)]
    input_grad, new_gain, new_gate, new_up, new_down = lax.switch(
        step_index[0] % level_count, branches,
        tokens[0], cotangent[0], gain, w_gate[0], w_up[0], w_down[0],
    )
    results = place_results(
        input_grad[None], new_gain, new_gate[None], new_up[None], new_down[None]
    )
    return tuple(results)


def place_results(*arrays):
    def body(*refs):
        n = len(refs) // 2
        sems = refs[-1]
        copies = [pltpu.make_async_copy(refs[i], refs[n + i], sems.at[i]) for i in range(n)]
        for copy in copies:
            copy.start()
        for copy in copies:
            copy.wait()

    anywhere = pl.BlockSpec(memory_space=pl.ANY)
    return pl.pallas_call(
        body,
        out_shape=tuple(jax.ShapeDtypeStruct(a.shape, a.dtype) for a in arrays),
        in_specs=[anywhere] * len(arrays),
        out_specs=(anywhere,) * len(arrays),
        scratch_shapes=[pltpu.SemaphoreType.DMA((len(arrays),))],
    )(*arrays)


def solution(mesh):
    in_specs = (
        P("rep", "fsdp", None),
        P("rep", "fsdp", None),
        P("rep", None),
        P("rep", None, "fsdp"),
        P("rep", None, "fsdp"),
        P("rep", "fsdp", None),
        P(),
    )
    out_specs = (
        P("rep", "fsdp", None),
        P("rep", None),
        P("rep", None, "fsdp"),
        P("rep", None, "fsdp"),
        P("rep", "fsdp", None),
    )
    return jax.shard_map(local, mesh=mesh, in_specs=in_specs, out_specs=out_specs, check_vma=False)
```
